32 devices in a mesh: groups: 2 (over y), patch: 8 (over z, x), uly: 2 (over core).
Axes of the slice: x: 2, y: 2, z: 4, core: 2. Of those that a mesh axis runs over, the one named last changes fastest.
Arguments:
- fresh_qkv: bfloat16 [1280, 3, 2560], P(('groups', 'patch', 'uly')), parts along dimension 0, may hold values from -40 to 40
- stale_kv: bfloat16 [1280, 2, 2560], P(('groups', 'patch'), None, 'uly'), parts along dimension 0, may hold values from -40 to 40
- q_gain: float32 [2560], replicated, may hold values from 0.5 to 1.5
- k_gain: float32 [2560], replicated, may hold values from 2 to 4
Outputs:
- attended: bfloat16 [1280, 2560], P(('groups', 'patch', 'uly')), parts along dimension 0
The draws below stay inside these ranges and needn't reach their ends.
There are 2 independent parts, one for each index of `groups`. The reference program is written for one: setup_inputs(seed, part) draws one part's arguments, and reference() takes and returns one part's arrays. A program takes and returns all parts, laid end to end along the dimension named above; an argument that names none is the same for every part. Nothing has to cross between parts.
All inputs are finite; a program needn't handle non-finite values.
Results may differ from the reference program's by a relative error of at most 0.0074.
Values may be sent and summed in bfloat16 or wider, within the bound.
No kernel may reach another device: no remote copies, remote signals or barrier semaphores. Data moves between devices by JAX's collectives and lax.ppermute only.
A program may use at most 128 MiB of HBM per device.

```python
import math
import jax
import jax.numpy as jnp
from jax import lax

HEADS = 20
HD = 128
PATCH_TOK = 80
TOKENS = 640
N_PATCH = 8


def draw_stale_kv(key, part):
    key = jax.random.fold_in(key, 1)
    first_key, second_key = jax.random.split(key, 2)
    key_part = jnp.clip(3.0 * jax.random.normal(first_key, (TOKENS, HEADS * HD), jnp.float32), -18.0, 18.0)
    value_part = jnp.clip(jax.random.normal(second_key, (TOKENS, HEADS * HD), jnp.float32), -6.0, 6.0)
    return jnp.stack([key_part, value_part], axis=1).astype(jnp.bfloat16)


def draw_fresh_qkv(key, part):
    key = jax.random.fold_in(key, 2)
    first_key = jax.random.fold_in(key, 0)
    triple = jnp.clip(jax.random.normal(first_key, (TOKENS, 3, HEADS * HD), jnp.float32), -6.0, 6.0)
    return triple.astype(jnp.bfloat16)


def setup_inputs(seed: int = 0, part: int = 0) -> dict:
    streams_of = jax.random.split(jax.random.key(seed), 5)
    part_splits = jax.random.split(jax.random.fold_in(streams_of[4], part), 5)
    return {
        "fresh_qkv": draw_fresh_qkv(jax.random.fold_in(jax.random.fold_in(streams_of[4], part), 71), part),
        "stale_kv": draw_stale_kv(jax.random.fold_in(jax.random.fold_in(streams_of[4], part), 71), part),
        "q_gain": jnp.clip(1.0 + 0.1 * jax.random.normal(streams_of[2], (HEADS * HD,), jnp.float32), 0.5, 1.5),
        "k_gain": jnp.clip(jax.random.uniform(streams_of[3], (HEADS * HD,), jnp.float32, 2.0, 4.0), 2.0, 4.0),
    }


EPSILON = 1e-06

def normalise(features, gain):
    features = features.astype(jnp.float32)
    mean_square = lax.optimization_barrier(jnp.mean(features * features, axis=-1, keepdims=True))
    return (features * lax.rsqrt(mean_square + EPSILON) * gain).astype(jnp.bfloat16)

def reference(fresh_qkv, stale_kv, q_gain, k_gain):
    queries = normalise(fresh_qkv[:, 0], q_gain)
    fresh_keys = normalise(fresh_qkv[:, 1], k_gain)
    fresh_values = fresh_qkv[:, 2]
    stale_keys = stale_kv[:, 0]
    stale_values = stale_kv[:, 1]
    score_scale = 1.0 / math.sqrt(HD)

    def one_patch(patch_index):
        first_row = (patch_index * PATCH_TOK).astype(jnp.int32)
        block_queries = lax.dynamic_slice_in_dim(queries, first_row, PATCH_TOK, 0)
        key_block = lax.dynamic_slice_in_dim(fresh_keys, first_row, PATCH_TOK, 0)
        value_block = lax.dynamic_slice_in_dim(fresh_values, first_row, PATCH_TOK, 0)
        all_keys = lax.dynamic_update_slice_in_dim(stale_keys, key_block, first_row, 0)
        all_values = lax.dynamic_update_slice_in_dim(stale_values, value_block, first_row, 0)
        query_heads = block_queries.astype(jnp.float32).reshape(PATCH_TOK, HEADS, HD)
        key_heads = all_keys.astype(jnp.float32).reshape(TOKENS, HEADS, HD)
        value_heads = all_values.astype(jnp.float32).reshape(TOKENS, HEADS, HD)
        scores = jnp.einsum('qhd,khd->hqk', query_heads, key_heads) * score_scale
        row_max = lax.optimization_barrier(jnp.max(scores, axis=-1, keepdims=True))
        weights = jnp.exp(scores - row_max)
        row_total = lax.optimization_barrier(jnp.sum(weights, axis=-1))
        rounded = lax.optimization_barrier(weights.astype(jnp.bfloat16)).astype(jnp.float32)
        summed = jnp.einsum('hqk,khd->hqd', rounded, value_heads) / row_total[..., None]
        return summed.transpose(1, 0, 2).reshape(PATCH_TOK, HEADS * HD).astype(jnp.bfloat16)
    blocks = lax.map(one_patch, jnp.arange(N_PATCH, dtype=jnp.int32))
    return blocks.reshape(TOKENS, HEADS * HD)
```

```python
import functools
import math

import jax
import jax.numpy as jnp
from jax import lax
from jax.experimental import pallas as pl
from jax.experimental.pallas import tpu as pltpu
from jax.sharding import PartitionSpec as P

HD = 128
EPSILON = 1e-06
SCALE = math.log2(math.e) / math.sqrt(HD)
VMEM = pl.BlockSpec(memory_space=pltpu.VMEM)
F32 = jnp.float32
BF16 = jnp.bfloat16


def call(body, outs, *args, flops=0, aliases=None):
    size = sum(a.size * a.dtype.itemsize for a in args) + sum(
        math.prod(s) * jnp.dtype(t).itemsize for s, t in outs
    )
    return pl.pallas_call(
        body,
        out_shape=[jax.ShapeDtypeStruct(s, t) for s, t in outs],
        in_specs=[VMEM] * len(args),
        out_specs=[VMEM] * len(outs),
        input_output_aliases=aliases or {},
        compiler_params=pltpu.CompilerParams(vmem_limit_bytes=32 << 20),
        cost_estimate=pl.CostEstimate(flops=flops, bytes_accessed=size, transcendentals=0),
    )(*args)


def split_kernel(x_ref, a_ref, b_ref):
    half = a_ref.shape[-1]
    for part in range(2):
        a_ref[part] = x_ref[:, part, :half]
        b_ref[part] = x_ref[:, part, half:]


def prep_kernel(x_ref, qg_ref, kg_ref, keep_ref, send_ref):
    width = keep_ref.shape[-1]
    first = lax.axis_index("uly") == 0

    def put(part, rows):
        low, high = rows[:, :width], rows[:, width:]

        @pl.when(first)
        def _():
            keep_ref[part] = low
            send_ref[part] = high

        @pl.when(jnp.logical_not(first))
        def _():
            keep_ref[part] = high
            send_ref[part] = low

    for part, gain in ((0, qg_ref), (1, kg_ref)):
        rows = x_ref[part].astype(F32)
        inverse = lax.rsqrt(jnp.mean(rows * rows, axis=-1, keepdims=True) + EPSILON)
        put(part, (rows * inverse * gain[...]).astype(BF16))
    put(2, x_ref[2])


def head_scores(query, key):
    return lax.dot_general(query, key, (((1,), (1,)), ((), ())), preferred_element_type=F32)


def both(one, two):
    return jnp.concatenate([one.astype(F32), two.astype(F32)], axis=0).astype(BF16)


def own_kernel(keep_ref, recv_ref, *outs):
    heads = outs[0].shape[-1] // HD
    for side in range(2):
        q_ref, acc_ref, ml_ref = outs[3 * side : 3 * side + 3]
        for head in range(heads):
            src = pl.ds((side * heads + head) * HD, HD)
            dst = pl.ds(head * HD, HD)
            query = both(keep_ref[0, :, src], recv_ref[0, :, src])
            key = both(keep_ref[1, :, src], recv_ref[1, :, src])
            value = both(keep_ref[2, :, src], recv_ref[2, :, src])
            q_ref[:, dst] = query
            scores = head_scores(query, key)
            best = jnp.max(scores, axis=-1, keepdims=True)
            weights = jnp.exp2((scores - best) * SCALE)
            ml_ref[0, :, head : head + 1] = best
            ml_ref[1, :, head : head + 1] = jnp.sum(weights, axis=-1, keepdims=True)
            acc_ref[:, dst] = jnp.dot(weights.astype(BF16), value, preferred_element_type=F32)


def head_update(head, q_ref, kv_refs, acc_ref, ml_ref):
    at = pl.ds(head * HD, HD)
    keys = [kv[0, :, at] for kv in kv_refs]
    values = [kv[1, :, at] for kv in kv_refs]
    key = keys[0] if len(keys) == 1 else jnp.concatenate(keys, axis=0)
    value = values[0] if len(values) == 1 else jnp.concatenate(values, axis=0)
    scores = head_scores(q_ref[:, at], key)
    old = ml_ref[0, :, head : head + 1]
    best = jnp.maximum(old, jnp.max(scores, axis=-1, keepdims=True))
    weights = jnp.exp2((scores - best) * SCALE)
    shrink = jnp.exp2((old - best) * SCALE)
    total = ml_ref[1, :, head : head + 1] * shrink + jnp.sum(weights, axis=-1, keepdims=True)
    acc = acc_ref[:, at] * shrink + jnp.dot(weights.astype(BF16), value, preferred_element_type=F32)
    return best, total, acc


def update_kernel(blocks, q_ref, *refs):
    kv_refs, (acc_ref, ml_ref, acc_out, ml_out) = refs[:blocks], refs[blocks:]
    for head in range(q_ref.shape[-1] // HD):
        best, total, acc = head_update(head, q_ref, kv_refs, acc_ref, ml_ref)
        ml_out[0, :, head : head + 1] = best
        ml_out[1, :, head : head + 1] = total
        acc_out[:, head * HD : (head + 1) * HD] = acc


def last_kernel(*refs):
    mine_ref, send_ref = refs[-2:]
    rows = mine_ref.shape[0]
    count = (len(refs) - 2) // 2
    for side in range(2):
        q_ref, acc_ref, ml_ref, *kv_refs = refs[side * count : (side + 1) * count]
        heads = q_ref.shape[-1] // HD
        for head in range(heads):
            _, total, acc = head_update(head, q_ref, kv_refs, acc_ref, ml_ref)
            out = acc / total
            at = pl.ds((side * heads + head) * HD, HD)
            mine_ref[:, at] = out[:rows].astype(BF16)
            send_ref[:, at] = out[rows:].astype(BF16)


def join_kernel(mine_ref, recv_ref, out_ref):
    width = mine_ref.shape[-1]
    first = lax.axis_index("uly") == 0

    @pl.when(first)
    def _():
        out_ref[:, :width] = mine_ref[...]
        out_ref[:, width:] = recv_ref[...]

    @pl.when(jnp.logical_not(first))
    def _():
        out_ref[:, :width] = recv_ref[...]
        out_ref[:, width:] = mine_ref[...]


def shards(n, fresh_qkv, stale_kv, q_gain, k_gain):
    rows, _, features = fresh_qkv.shape
    patch_rows, _, width = stale_kv.shape
    half = width // 2
    around = list(range(0, n, 2)) + list(range(1, n, 2))[::-1]
    right = [(around[i], around[(i + 1) % n]) for i in range(n)]
    left = [(b, a) for a, b in right]
    swap = [(0, 1), (1, 0)]
    far, near = n // 2, (n - 1) // 2

    sides = call(split_kernel, [((2, patch_rows, half), BF16)] * 2, stale_kv)
    forward, backward = list(sides), list(sides)
    arrived = [[], []]
    for hop in range(max(far, near)):
        for side in range(2):
            got = []
            if hop < (far if side == 0 else near):
                forward[side] = lax.ppermute(forward[side], "patch", right)
                got.append(forward[side])
            if hop < (near if side == 0 else far):
                backward[side] = lax.ppermute(backward[side], "patch", left)
                got.append(backward[side])
            arrived[side].append(got)

    keep, send = call(
        prep_kernel,
        [((3, rows, width), BF16)] * 2,
        fresh_qkv.transpose(1, 0, 2),
        q_gain.reshape(1, features),
        k_gain.reshape(1, features),
    )
    recv = lax.ppermute(send, "uly", swap)
    state = [((patch_rows, half), BF16), ((patch_rows, half), F32), ((2, patch_rows, HD), F32)]
    own = call(own_kernel, state * 2, keep, recv, flops=4 * patch_rows * patch_rows * width)
    states = [own[:3], own[3:]]
    hops = len(arrived[0])
    for hop in range(hops - 1):
        for side in range(2):
            blocks = arrived[side][hop]
            query, acc, ml = states[side]
            k = len(blocks)
            acc, ml = call(
                functools.partial(update_kernel, k),
                state[1:],
                query,
                *blocks,
                acc,
                ml,
                flops=4 * k * patch_rows * patch_rows * half,
                aliases={k + 1: 0, k + 2: 1},
            )
            states[side] = [query, acc, ml]
    mine, outgoing = call(
        last_kernel,
        [((rows, width), BF16)] * 2,
        *states[0],
        *arrived[0][-1],
        *states[1],
        *arrived[1][-1],
        flops=4 * patch_rows * patch_rows * width,
    )
    incoming = lax.ppermute(outgoing, "uly", swap)
    (out,) = call(join_kernel, [((rows, features), BF16)], mine, incoming)
    return out


def solution(mesh):
    in_specs = (
        P(("groups", "patch", "uly"), None, None),
        P(("groups", "patch"), None, "uly"),
        P(),
        P(),
    )
    out_specs = P(("groups", "patch", "uly"), None)
    body = functools.partial(shards, mesh.shape["patch"])
    return jax.shard_map(body, mesh=mesh, in_specs=in_specs, out_specs=out_specs, check_vma=False)
```

```python
import functools
import math

import jax
import jax.numpy as jnp
from jax import lax
from jax.experimental import pallas as pl
from jax.experimental.pallas import tpu as pltpu
from jax.sharding import PartitionSpec as P

HD = 128
EPSILON = 1e-06
SCALE = math.log2(math.e) / math.sqrt(HD)
VMEM = pl.BlockSpec(memory_space=pltpu.VMEM)
ANY = pl.BlockSpec(memory_space=pl.ANY)
F32 = jnp.float32
BF16 = jnp.bfloat16
WORK = 24
OWN = 1
GRANT = 32 << 20


def call(name, body, outs, *args, flops=0, ins=None, to=None, aliases=None, scratch=(), grant=32 << 20):
    size = sum(a.size * a.dtype.itemsize for a in args) + sum(
        math.prod(s) * jnp.dtype(t).itemsize for s, t in outs
    )
    return pl.pallas_call(
        body,
        name=name,
        out_shape=[jax.ShapeDtypeStruct(s, t) for s, t in outs],
        in_specs=ins or [VMEM] * len(args),
        out_specs=to or [VMEM] * len(outs),
        scratch_shapes=scratch,
        input_output_aliases=aliases or {},
        compiler_params=pltpu.CompilerParams(vmem_limit_bytes=grant),
        cost_estimate=pl.CostEstimate(flops=flops, bytes_accessed=size, transcendentals=0),
    )(*args)


def split_kernel(side, x_hbm, out_ref, buf, sem):
    half = out_ref.shape[-1]
    copy = pltpu.make_async_copy(x_hbm.at[:, :, pl.ds(side * half, half)], buf, sem)
    copy.start()
    copy.wait()
    for part in range(2):
        out_ref[part] = buf[:, part]


def prep_kernel(x_hbm, qg_ref, kg_ref, _, __, keep_ref, send_ref, buf, sem):
    width = keep_ref.shape[-1]
    first = lax.axis_index("uly") == 0
    copies = [pltpu.make_async_copy(x_hbm.at[i], buf.at[i], sem.at[i]) for i in range(3)]
    for copy in copies:
        copy.start()

    def put(part, rows):
        low, high = rows[:, :width], rows[:, width:]

        @pl.when(first)
        def _():
            keep_ref[part] = low
            send_ref[part] = high

        @pl.when(jnp.logical_not(first))
        def _():
            keep_ref[part] = high
            send_ref[part] = low

    for part, gain in ((0, qg_ref), (1, kg_ref)):
        copies[part].wait()
        rows = buf[part].astype(F32)
        inverse = lax.rsqrt(jnp.mean(rows * rows, axis=-1, keepdims=True) + EPSILON)
        put(part, (rows * inverse * gain[...]).astype(BF16))
    copies[2].wait()
    put(2, buf[2])


def scores_of(query, key):
    return lax.dot_general(query, key, (((1,), (1,)), ((), ())), preferred_element_type=F32)


def both(one, two):
    return jnp.concatenate([one.astype(F32), two.astype(F32)], axis=0).astype(BF16)


def own_kernel(keep_ref, recv_ref, *outs):
    heads = outs[0].shape[-1] // HD
    for side in range(2):
        q_ref, acc_ref, best_ref, total_ref = outs[4 * side : 4 * side + 4]
        for head in range(heads):
            src = pl.ds((side * heads + head) * HD, HD)
            dst = pl.ds(head * HD, HD)
            query = both(keep_ref[0, :, src], recv_ref[0, :, src])
            key = both(keep_ref[1, :, src], recv_ref[1, :, src])
            value = both(keep_ref[2, :, src], recv_ref[2, :, src])
            scores = scores_of(query, key)
            best = jnp.max(scores, axis=-1, keepdims=True)
            weights = jnp.exp2((scores - best) * SCALE)
            total = jnp.sum(weights, axis=-1, keepdims=True)
            acc = jnp.dot(weights.astype(BF16), value, preferred_element_type=F32)
            q_ref[:, dst] = query
            best_ref[:, dst] = jnp.broadcast_to(best, acc.shape)
            total_ref[:, dst] = jnp.broadcast_to(total, acc.shape)
            acc_ref[:, dst] = acc


def step(query, keys, values, acc, old, total):
    scores = [scores_of(query, key) for key in keys]
    top = jnp.max(functools.reduce(jnp.maximum, scores), axis=-1, keepdims=True)
    best = jnp.maximum(old, jnp.broadcast_to(top, old.shape))
    shrink = jnp.exp2((old - best) * SCALE)
    weights = [jnp.exp2((s - best[:, : s.shape[-1]]) * SCALE) for s in scores]
    total = total * shrink + jnp.sum(functools.reduce(jnp.add, weights), axis=-1, keepdims=True)
    acc = acc * shrink
    for w, value in zip(weights, values):
        acc = acc + jnp.dot(w.astype(BF16), value, preferred_element_type=F32)
    return acc, best, total


def update_kernel(blocks, q_ref, *refs):
    kv_refs, state, outs = refs[:blocks], refs[blocks : blocks + 3], refs[blocks + 3 :]
    for head in range(q_ref.shape[-1] // HD):
        at = pl.ds(head * HD, HD)
        old = [ref[:, at] for ref in state]
        keys = [kv[0, :, at] for kv in kv_refs]
        values = [kv[1, :, at] for kv in kv_refs]
        new = step(q_ref[:, at], keys, values, *old)
        for ref, value in zip(outs, new):
            ref[:, at] = value


def finish(begin, q_ref, sides, put):
    rows = q_ref.shape[1]
    for side, (acc_ref, best_ref, total_ref, *kv_refs) in enumerate(sides):
        heads = acc_ref.shape[-1] // HD
        for head in range(heads):
            at = pl.ds(head * HD, HD)
            to = pl.ds((side * heads + head) * HD, HD)
            old = [ref[begin : begin + rows, at] for ref in (acc_ref, best_ref, total_ref)]
            keys = [kv[0, :, at] for kv in kv_refs]
            values = [kv[1, :, at] for kv in kv_refs]
            acc, _, total = step(q_ref[0, :, to], keys, values, *old)
            put(to, (acc / total).astype(BF16))


def send_kernel(begin, cut, q_ref, *refs):
    out_ref = refs[-1]

    def put(to, value):
        out_ref[:, to] = value

    finish(begin, q_ref, (refs[:cut], refs[cut:-1]), put)


def mine_kernel(begin, cut, q_ref, *refs):
    out_hbm, buf, sem = refs[-3:]

    def put(to, value):
        buf[:, to] = value

    finish(begin, q_ref, (refs[:cut], refs[cut:-3]), put)
    width = buf.shape[-1]
    at = pl.ds(pl.multiple_of(lax.axis_index("uly") * width, HD), width)
    copy = pltpu.make_async_copy(buf, out_hbm.at[:, at], sem)
    copy.start()
    copy.wait()


def join_kernel(recv_ref, _, out_hbm, sem):
    width = recv_ref.shape[-1]
    at = pl.ds(pl.multiple_of((1 - lax.axis_index("uly")) * width, HD), width)
    copy = pltpu.make_async_copy(recv_ref, out_hbm.at[:, at], sem)
    copy.start()
    copy.wait()


def shards(n, fresh_qkv, stale_kv, q_gain, k_gain):
    rows, _, features = fresh_qkv.shape
    patch_rows, _, width = stale_kv.shape
    half = width // 2
    around = list(range(0, n, 2)) + list(range(1, n, 2))[::-1]
    right = [(around[i], around[(i + 1) % n]) for i in range(n)]
    left = [(b, a) for a, b in right]
    swap = [(0, 1), (1, 0)]
    far, near = n // 2, (n - 1) // 2

    dma = pltpu.SemaphoreType.DMA
    sides = [
        call(
            f"split{side}",
            functools.partial(split_kernel, side),
            [((2, patch_rows, half), BF16)],
            stale_kv,
            ins=[ANY],
            scratch=[pltpu.VMEM((patch_rows, 2, half), BF16), dma],
            grant=GRANT,
        )[0]
        for side in range(2)
    ]
    forward, backward = list(sides), list(sides)
    arrived = [[], []]
    for hop in range(max(far, near)):
        for side in range(2):
            got = []
            if hop < (far if side == 0 else near):
                forward[side] = lax.ppermute(forward[side], "patch", right)
                got.append(forward[side])
            if hop < (near if side == 0 else far):
                backward[side] = lax.ppermute(backward[side], "patch", left)
                got.append(backward[side])
            arrived[side].append(got)

    keep, send = call(
        "prep",
        prep_kernel,
        [((3, rows, width), BF16)] * 2,
        fresh_qkv.transpose(1, 0, 2),
        q_gain.reshape(1, features),
        k_gain.reshape(1, features),
        *sides,
        ins=[ANY, VMEM, VMEM, ANY, ANY],
        scratch=[pltpu.VMEM((3, rows, features), BF16), dma((3,))],
        grant=GRANT,
        flops=patch_rows * patch_rows * width // 8,
    )
    recv = lax.ppermute(send, "uly", swap)
    state = [((patch_rows, half), F32)] * 3
    work = WORK * 4 * patch_rows * patch_rows * half
    own = call("own", own_kernel, ([((patch_rows, half), BF16)] + state) * 2, keep, recv, flops=OWN * work)
    queries = [own[0], own[4]]
    states = [own[1:4], own[5:8]]
    for hop in range(len(arrived[0]) - 1):
        for side in range(2):
            blocks = arrived[side][hop]
            body = functools.partial(update_kernel, len(blocks))
            states[side] = call(
                f"update{hop}{side}", body, state, queries[side], *blocks, *states[side], flops=len(blocks) * work
            )
    last = [*states[0], *arrived[0][-1], *states[1], *arrived[1][-1]]
    cut = len(states[0]) + len(arrived[0][-1])
    (outgoing,) = call(
        "send", functools.partial(send_kernel, rows, cut), [((rows, width), BF16)], recv, *last, flops=work
    )
    incoming = lax.ppermute(outgoing, "uly", swap)
    result = [((rows, features), BF16)]
    (out,) = call(
        "mine",
        functools.partial(mine_kernel, 0, cut),
        result,
        keep,
        *last,
        to=[ANY],
        scratch=[pltpu.VMEM((rows, width), BF16), dma],
        flops=work,
    )
    (out,) = call("join", join_kernel, result, incoming, out, ins=[VMEM, ANY], to=[ANY], aliases={1: 0}, scratch=[dma])
    return out


def solution(mesh):
    in_specs = (
        P(("groups", "patch", "uly"), None, None),
        P(("groups", "patch"), None, "uly"),
        P(),
        P(),
    )
    out_specs = P(("groups", "patch", "uly"), None)
    body = functools.partial(shards, mesh.shape["patch"])
    return jax.shard_map(body, mesh=mesh, in_specs=in_specs, out_specs=out_specs, check_vma=False)
```

```python
import functools
import math

import jax
import jax.numpy as jnp
from jax import lax
from jax.experimental import pallas as pl
from jax.experimental.pallas import tpu as pltpu
from jax.sharding import PartitionSpec as P

HD = 128
EPSILON = 1e-06
SCALE = math.log2(math.e) / math.sqrt(HD)
VMEM = pl.BlockSpec(memory_space=pltpu.VMEM)
ANY = pl.BlockSpec(memory_space=pl.ANY)
F32 = jnp.float32
BF16 = jnp.bfloat16
WORK = 24
OWN = 1
GRANT = 56150240
PIECES = 5


def call(name, body, outs, *args, flops=0, ins=None, to=None, aliases=None, scratch=(), grant=32 << 20):
    size = sum(a.size * a.dtype.itemsize for a in args) + sum(
        math.prod(s) * jnp.dtype(t).itemsize for s, t in outs
    )
    return pl.pallas_call(
        body,
        name=name,
        out_shape=[jax.ShapeDtypeStruct(s, t) for s, t in outs],
        in_specs=ins or [VMEM] * len(args),
        out_specs=to or [VMEM] * len(outs),
        scratch_shapes=scratch,
        input_output_aliases=aliases or {},
        compiler_params=pltpu.CompilerParams(vmem_limit_bytes=grant),
        cost_estimate=pl.CostEstimate(flops=flops, bytes_accessed=size, transcendentals=0),
    )(*args)


def split_kernel(side, x_hbm, out_ref, buf, sem):
    half = out_ref.shape[-1]
    count = sem.shape[0]
    rows = buf.shape[0] // count
    copies = []
    for i in range(count):
        at = pl.ds(i * rows, rows)
        copies.append(
            pltpu.make_async_copy(x_hbm.at[at, :, pl.ds(side * half, half)], buf.at[at], sem.at[i])
        )
        copies[i].start()
    for i in range(count):
        copies[i].wait()
        for part in range(2):
            out_ref[part, i * rows : (i + 1) * rows] = buf[i * rows : (i + 1) * rows, part]


def prep_kernel(x_hbm, qg_ref, kg_ref, _, __, keep_ref, send_ref, buf, sem):
    width = keep_ref.shape[-1]
    first = lax.axis_index("uly") == 0
    copies = [pltpu.make_async_copy(x_hbm.at[i], buf.at[i], sem.at[i]) for i in range(3)]
    for copy in copies:
        copy.start()

    def put(part, rows):
        low, high = rows[:, :width], rows[:, width:]

        @pl.when(first)
        def _():
            keep_ref[part] = low
            send_ref[part] = high

        @pl.when(jnp.logical_not(first))
        def _():
            keep_ref[part] = high
            send_ref[part] = low

    for part, gain in ((0, qg_ref), (1, kg_ref)):
        copies[part].wait()
        rows = buf[part].astype(F32)
        inverse = lax.rsqrt(jnp.mean(rows * rows, axis=-1, keepdims=True) + EPSILON)
        put(part, (rows * inverse * gain[...]).astype(BF16))
    copies[2].wait()
    put(2, buf[2])


def scores_of(query, key):
    return lax.dot_general(query, key, (((1,), (1,)), ((), ())), preferred_element_type=F32)


def both(one, two):
    return jnp.concatenate([one.astype(F32), two.astype(F32)], axis=0).astype(BF16)


def weigh(scores, old):
    top = jnp.max(functools.reduce(jnp.maximum, scores), axis=-1, keepdims=True)
    if old is None:
        weights = [jnp.exp2((s - top) * SCALE) for s in scores]
        total = jnp.sum(functools.reduce(jnp.add, weights), axis=-1, keepdims=True)
        shape = (top.shape[0], HD)
        return weights, None, jnp.broadcast_to(top, shape), jnp.broadcast_to(total, shape)
    _, best, total = old
    new = jnp.maximum(best, jnp.broadcast_to(top, best.shape))
    shrink = jnp.exp2((best - new) * SCALE)
    weights = [jnp.exp2((s - new[:, : s.shape[-1]]) * SCALE) for s in scores]
    total = total * shrink + jnp.sum(functools.reduce(jnp.add, weights), axis=-1, keepdims=True)
    return weights, shrink, new, total


def attend(heads):
    scores = [[scores_of(query, key) for key in keys] for query, keys, _, _ in heads]
    weighed = [weigh(s, old) for s, (_, _, _, old) in zip(scores, heads)]
    for (_, _, values, old), (weights, shrink, best, total) in zip(heads, weighed):
        products = [
            jnp.dot(w.astype(BF16), value, preferred_element_type=F32)
            for w, value in zip(weights, values)
        ]
        acc = functools.reduce(jnp.add, products)
        yield (acc if old is None else old[0] * shrink + acc), best, total


def own_kernel(keep_ref, recv_ref, *outs):
    count = outs[0].shape[-1] // HD
    heads = []
    for head in range(2 * count):
        at = pl.ds(head * HD, HD)
        query, key, value = (both(keep_ref[i, :, at], recv_ref[i, :, at]) for i in range(3))
        heads.append((query, [key], [value], None))
    for head, new in enumerate(attend(heads)):
        q_ref, *state = outs[4 * (head // count) : 4 * (head // count) + 4]
        to = pl.ds(head % count * HD, HD)
        q_ref[:, to] = heads[head][0]
        for ref, value in zip(state, new):
            ref[:, to] = value


def update_kernel(blocks, q_ref, *refs):
    kv_refs, state, outs = refs[:blocks], refs[blocks : blocks + 3], refs[blocks + 3 :]
    heads = []
    for head in range(q_ref.shape[-1] // HD):
        at = pl.ds(head * HD, HD)
        keys, values = ([kv[i, :, at] for kv in kv_refs] for i in range(2))
        heads.append((q_ref[:, at], keys, values, [ref[:, at] for ref in state]))
    for head, new in enumerate(attend(heads)):
        for ref, value in zip(outs, new):
            ref[:, head * HD : (head + 1) * HD] = value


def finish(begin, q_ref, sides, out_ref):
    rows = q_ref.shape[1]
    heads = []
    for *state, kv_refs in sides:
        for head in range(state[0].shape[-1] // HD):
            at = pl.ds(head * HD, HD)
            query = q_ref[0, :, pl.ds(len(heads) * HD, HD)]
            keys, values = ([kv[i, :, at] for kv in kv_refs] for i in range(2))
            old = [ref[begin : begin + rows, at] for ref in state]
            heads.append((query, keys, values, old))
    for head, (acc, _, total) in enumerate(attend(heads)):
        out_ref[:, head * HD : (head + 1) * HD] = (acc / total).astype(BF16)


def two_sides(refs, cut):
    return [(*side[:3], side[3:]) for side in (refs[:cut], refs[cut:])]


def send_kernel(begin, cut, q_ref, *refs):
    finish(begin, q_ref, two_sides(refs[:-1], cut), refs[-1])


def mine_kernel(begin, cut, q_ref, *refs):
    out_hbm, buf, sem = refs[-3:]
    finish(begin, q_ref, two_sides(refs[:-3], cut), buf)
    width = buf.shape[-1]
    at = pl.ds(pl.multiple_of(lax.axis_index("uly") * width, HD), width)
    copy = pltpu.make_async_copy(buf, out_hbm.at[:, at], sem)
    copy.start()
    copy.wait()


def join_kernel(recv_ref, _, out_hbm, sem):
    width = recv_ref.shape[-1]
    at = pl.ds(pl.multiple_of((1 - lax.axis_index("uly")) * width, HD), width)
    copy = pltpu.make_async_copy(recv_ref, out_hbm.at[:, at], sem)
    copy.start()
    copy.wait()


def shards(n, fresh_qkv, stale_kv, q_gain, k_gain):
    rows, _, features = fresh_qkv.shape
    patch_rows, _, width = stale_kv.shape
    half = width // 2
    around = list(range(0, n, 2)) + list(range(1, n, 2))[::-1]
    right = [(around[i], around[(i + 1) % n]) for i in range(n)]
    left = [(b, a) for a, b in right]
    swap = [(0, 1), (1, 0)]
    far, near = n // 2, (n - 1) // 2

    dma = pltpu.SemaphoreType.DMA
    sides = [
        call(
            f"split{side}",
            functools.partial(split_kernel, side),
            [((2, patch_rows, half), BF16)],
            stale_kv,
            ins=[ANY],
            scratch=[pltpu.VMEM((patch_rows, 2, half), BF16), dma((PIECES,))],
            grant=GRANT,
        )[0]
        for side in range(2)
    ]
    forward, backward = list(sides), list(sides)
    arrived = [[], []]
    for hop in range(max(far, near)):
        for side in range(2):
            got = []
            if hop < (far if side == 0 else near):
                forward[side] = lax.ppermute(forward[side], "patch", right)
                got.append(forward[side])
            if hop < (near if side == 0 else far):
                backward[side] = lax.ppermute(backward[side], "patch", left)
                got.append(backward[side])
            arrived[side].append(got)

    keep, send = call(
        "prep",
        prep_kernel,
        [((3, rows, width), BF16)] * 2,
        fresh_qkv.transpose(1, 0, 2),
        q_gain.reshape(1, features),
        k_gain.reshape(1, features),
        *sides,
        ins=[ANY, VMEM, VMEM, ANY, ANY],
        scratch=[pltpu.VMEM((3, rows, features), BF16), dma((3,))],
        flops=patch_rows * patch_rows * width // 8,
    )
    recv = lax.ppermute(send, "uly", swap)
    state = [((patch_rows, half), F32)] * 3
    work = WORK * 4 * patch_rows * patch_rows * half
    own = call("own", own_kernel, ([((patch_rows, half), BF16)] + state) * 2, keep, recv, flops=OWN * work)
    queries = [own[0], own[4]]
    states = [own[1:4], own[5:8]]
    for hop in range(len(arrived[0]) - 1):
        for side in range(2):
            blocks = arrived[side][hop]
            body = functools.partial(update_kernel, len(blocks))
            states[side] = call(
                f"update{hop}{side}", body, state, queries[side], *blocks, *states[side], flops=len(blocks) * work
            )
    last = [*states[0], *arrived[0][-1], *states[1], *arrived[1][-1]]
    cut = len(states[0]) + len(arrived[0][-1])
    (outgoing,) = call(
        "send", functools.partial(send_kernel, rows, cut), [((rows, width), BF16)], recv, *last, flops=work
    )
    incoming = lax.ppermute(outgoing, "uly", swap)
    result = [((rows, features), BF16)]
    (out,) = call(
        "mine",
        functools.partial(mine_kernel, 0, cut),
        result,
        keep,
        *last,
        to=[ANY],
        scratch=[pltpu.VMEM((rows, width), BF16), dma],
        flops=work,
    )
    (out,) = call("join", join_kernel, result, incoming, out, ins=[VMEM, ANY], to=[ANY], aliases={1: 0}, scratch=[dma])
    return out


def solution(mesh):
    in_specs = (
        P(("groups", "patch", "uly"), None, None),
        P(("groups", "patch"), None, "uly"),
        P(),
        P(),
    )
    out_specs = P(("groups", "patch", "uly"), None)
    body = functools.partial(shards, mesh.shape["patch"])
    return jax.shard_map(body, mesh=mesh, in_specs=in_specs, out_specs=out_specs, check_vma=False)
```

```python
import functools
import math

import jax
import jax.numpy as jnp
from jax import lax
from jax.experimental import pallas as pl
from jax.experimental.pallas import tpu as pltpu
from jax.sharding import PartitionSpec as P

HD = 128
EPSILON = 1e-06
SCALE = math.log2(math.e) / math.sqrt(HD)
VMEM = pl.BlockSpec(memory_space=pltpu.VMEM)
ANY = pl.BlockSpec(memory_space=pl.ANY)
F32 = jnp.float32
BF16 = jnp.bfloat16
WORK = 1
OWN = 1
LATE = 1
PREP = 1
BYTES = 1
GRANT = 55900000
PIECES = 5


def call(name, body, outs, *args, flops=0, ins=None, to=None, aliases=None, scratch=(), grant=32 << 20):
    size = sum(a.size * a.dtype.itemsize for a in args) + sum(
        math.prod(s) * jnp.dtype(t).itemsize for s, t in outs
    )
    return pl.pallas_call(
        body,
        name=name,
        out_shape=[jax.ShapeDtypeStruct(s, t) for s, t in outs],
        in_specs=ins or [VMEM] * len(args),
        out_specs=to or [VMEM] * len(outs),
        scratch_shapes=scratch,
        input_output_aliases=aliases or {},
        compiler_params=pltpu.CompilerParams(vmem_limit_bytes=grant),
        cost_estimate=pl.CostEstimate(flops=int(flops), bytes_accessed=int(size * BYTES), transcendentals=0),
    )(*args)


def load_kernel(x_hbm, *refs):
    outs, sem = refs[:2], refs[2]
    half = outs[0].shape[-1]
    copies = []
    for side in range(2):
        at = pl.ds(side * half, half)
        copies.append(pltpu.make_async_copy(x_hbm.at[:, :, at], outs[side], sem.at[side]))
        copies[side].start()
    for copy in copies:
        copy.wait()


def part_kernel(x_ref, out_ref):
    for part in range(2):
        out_ref[part] = x_ref[:, part]


def prep_kernel(x_hbm, qg_ref, kg_ref, _, __, keep_ref, send_ref, buf, sem):
    width = keep_ref.shape[-1]
    first = lax.axis_index("uly") == 0
    copies = [pltpu.make_async_copy(x_hbm.at[i], buf.at[i], sem.at[i]) for i in range(3)]
    for copy in copies:
        copy.start()

    def put(part, rows):
        low, high = rows[:, :width], rows[:, width:]

        @pl.when(first)
        def _():
            keep_ref[part] = low
            send_ref[part] = high

        @pl.when(jnp.logical_not(first))
        def _():
            keep_ref[part] = high
            send_ref[part] = low

    for part, gain in ((0, qg_ref), (1, kg_ref)):
        copies[part].wait()
        rows = buf[part].astype(F32)
        inverse = lax.rsqrt(jnp.mean(rows * rows, axis=-1, keepdims=True) + EPSILON)
        put(part, (rows * inverse * gain[...]).astype(BF16))
    copies[2].wait()
    put(2, buf[2])


def scores_of(query, key):
    return lax.dot_general(query, key, (((1,), (1,)), ((), ())), preferred_element_type=F32)


def both(one, two):
    return jnp.concatenate([one.astype(F32), two.astype(F32)], axis=0).astype(BF16)


def weigh(scores, old):
    top = jnp.max(functools.reduce(jnp.maximum, scores), axis=-1, keepdims=True)
    if old is None:
        weights = [jnp.exp2((s - top) * SCALE) for s in scores]
        total = jnp.sum(functools.reduce(jnp.add, weights), axis=-1, keepdims=True)
        shape = (top.shape[0], HD)
        return weights, None, jnp.broadcast_to(top, shape), jnp.broadcast_to(total, shape)
    _, best, total = old
    new = jnp.maximum(best, jnp.broadcast_to(top, best.shape))
    shrink = jnp.exp2((best - new) * SCALE)
    weights = [jnp.exp2((s - new[:, : s.shape[-1]]) * SCALE) for s in scores]
    total = total * shrink + jnp.sum(functools.reduce(jnp.add, weights), axis=-1, keepdims=True)
    return weights, shrink, new, total


def attend(heads):
    scores = [[scores_of(query, key) for key in keys] for query, keys, _, _ in heads]
    weighed = [weigh(s, old) for s, (_, _, _, old) in zip(scores, heads)]
    for (_, _, values, old), (weights, shrink, best, total) in zip(heads, weighed):
        products = [
            jnp.dot(w.astype(BF16), value, preferred_element_type=F32)
            for w, value in zip(weights, values)
        ]
        acc = functools.reduce(jnp.add, products)
        yield (acc if old is None else old[0] * shrink + acc), best, total


def own_kernel(keep_ref, recv_ref, *outs):
    count = outs[0].shape[-1] // HD
    heads = []
    for head in range(2 * count):
        at = pl.ds(head * HD, HD)
        query, key, value = (both(keep_ref[i, :, at], recv_ref[i, :, at]) for i in range(3))
        heads.append((query, [key], [value], None))
    for head, new in enumerate(attend(heads)):
        q_ref, *state = outs[4 * (head // count) : 4 * (head // count) + 4]
        to = pl.ds(head % count * HD, HD)
        q_ref[:, to] = heads[head][0]
        for ref, value in zip(state, new):
            ref[:, to] = value


def update_kernel(blocks, q_ref, *refs):
    kv_refs, state, outs = refs[:blocks], refs[blocks : blocks + 3], refs[blocks + 3 :]
    heads = []
    for head in range(q_ref.shape[-1] // HD):
        at = pl.ds(head * HD, HD)
        keys, values = ([kv[i, :, at] for kv in kv_refs] for i in range(2))
        heads.append((q_ref[:, at], keys, values, [ref[:, at] for ref in state]))
    for head, new in enumerate(attend(heads)):
        for ref, value in zip(outs, new):
            ref[:, head * HD : (head + 1) * HD] = value


def finish(begin, q_ref, sides, out_ref):
    rows = q_ref.shape[1]
    heads = []
    for *state, kv_refs in sides:
        for head in range(state[0].shape[-1] // HD):
            at = pl.ds(head * HD, HD)
            query = q_ref[0, :, pl.ds(len(heads) * HD, HD)]
            keys, values = ([kv[i, :, at] for kv in kv_refs] for i in range(2))
            old = [ref[begin : begin + rows, at] for ref in state]
            heads.append((query, keys, values, old))
    for head, (acc, _, total) in enumerate(attend(heads)):
        out_ref[:, head * HD : (head + 1) * HD] = (acc / total).astype(BF16)


def two_sides(refs, cut):
    return [(*side[:3], side[3:]) for side in (refs[:cut], refs[cut:])]


def send_kernel(begin, cut, q_ref, *refs):
    finish(begin, q_ref, two_sides(refs[:-1], cut), refs[-1])


def mine_kernel(begin, cut, q_ref, *refs):
    out_hbm, buf, sem = refs[-3:]
    finish(begin, q_ref, two_sides(refs[:-3], cut), buf)
    width = buf.shape[-1]
    at = pl.ds(pl.multiple_of(lax.axis_index("uly") * width, HD), width)
    copy = pltpu.make_async_copy(buf, out_hbm.at[:, at], sem)
    copy.start()
    copy.wait()


def join_kernel(recv_ref, _, out_hbm, sem):
    width = recv_ref.shape[-1]
    at = pl.ds(pl.multiple_of((1 - lax.axis_index("uly")) * width, HD), width)
    copy = pltpu.make_async_copy(recv_ref, out_hbm.at[:, at], sem)
    copy.start()
    copy.wait()


def shards(n, fresh_qkv, stale_kv, q_gain, k_gain):
    rows, _, features = fresh_qkv.shape
    patch_rows, _, width = stale_kv.shape
    half = width // 2
    around = list(range(0, n, 2)) + list(range(1, n, 2))[::-1]
    right = [(around[i], around[(i + 1) % n]) for i in range(n)]
    left = [(b, a) for a, b in right]
    swap = [(0, 1), (1, 0)]
    far, near = n // 2, (n - 1) // 2

    dma = pltpu.SemaphoreType.DMA
    sides = call(
        "load",
        load_kernel,
        [((patch_rows, 2, half), BF16)] * 2,
        stale_kv,
        ins=[ANY],
        scratch=[dma((2,))],
        grant=GRANT,
    )
    forward, backward = list(sides), list(sides)
    arrived = [[], []]
    def move(block, hop, way):
        block = lax.ppermute(block, "patch", way)
        return call("part", part_kernel, [((2, patch_rows, half), BF16)], block)[0] if hop == 0 else block

    for hop in range(max(far, near)):
        for side in range(2):
            got = []
            if hop < (far if side == 0 else near):
                forward[side] = move(forward[side], hop, right)
                got.append(forward[side])
            if hop < (near if side == 0 else far):
                backward[side] = move(backward[side], hop, left)
                got.append(backward[side])
            arrived[side].append(got)

    keep, send = call(
        "prep",
        prep_kernel,
        [((3, rows, width), BF16)] * 2,
        fresh_qkv.transpose(1, 0, 2),
        q_gain.reshape(1, features),
        k_gain.reshape(1, features),
        *sides,
        ins=[ANY, VMEM, VMEM, ANY, ANY],
        scratch=[pltpu.VMEM((3, rows, features), BF16), dma((3,))],
        flops=PREP * patch_rows * patch_rows * width // 8,
    )
    recv = lax.ppermute(send, "uly", swap)
    state = [((patch_rows, half), F32)] * 3
    work = WORK * 4 * patch_rows * patch_rows * half
    own = call("own", own_kernel, ([((patch_rows, half), BF16)] + state) * 2, keep, recv, flops=OWN * work)
    queries = [own[0], own[4]]
    states = [own[1:4], own[5:8]]
    for hop in range(len(arrived[0]) - 1):
        for side in range(2):
            blocks = arrived[side][hop]
            body = functools.partial(update_kernel, len(blocks))
            states[side] = call(
                f"update{hop}{side}", body, state, queries[side], *blocks, *states[side], flops=len(blocks) * (work if hop < len(arrived[0]) - 2 else LATE * work)
            )
    last = [*states[0], *arrived[0][-1], *states[1], *arrived[1][-1]]
    cut = len(states[0]) + len(arrived[0][-1])
    (outgoing,) = call(
        "send", functools.partial(send_kernel, rows, cut), [((rows, width), BF16)], recv, *last, flops=work
    )
    incoming = lax.ppermute(outgoing, "uly", swap)
    result = [((rows, features), BF16)]
    (out,) = call(
        "mine",
        functools.partial(mine_kernel, 0, cut),
        result,
        keep,
        *last,
        to=[ANY],
        scratch=[pltpu.VMEM((rows, width), BF16), dma],
        flops=work,
    )
    (out,) = call("join", join_kernel, result, incoming, out, ins=[VMEM, ANY], to=[ANY], aliases={1: 0}, scratch=[dma])
    return out


def solution(mesh):
    in_specs = (
        P(("groups", "patch", "uly"), None, None),
        P(("groups", "patch"), None, "uly"),
        P(),
        P(),
    )
    out_specs = P(("groups", "patch", "uly"), None)
    body = functools.partial(shards, mesh.shape["patch"])
    return jax.shard_map(body, mesh=mesh, in_specs=in_specs, out_specs=out_specs, check_vma=False)
```

```python
import functools
import math

import jax
import jax.numpy as jnp
from jax import lax
from jax.experimental import pallas as pl
from jax.experimental.pallas import tpu as pltpu
from jax.sharding import PartitionSpec as P

HD = 128
EPSILON = 1e-06
SCALE = math.log2(math.e) / math.sqrt(HD)
VMEM = pl.BlockSpec(memory_space=pltpu.VMEM)
ANY = pl.BlockSpec(memory_space=pl.ANY)
F32 = jnp.float32
BF16 = jnp.bfloat16
WORK = 1
OWN = 1
LATE = 1
PREP = 1
BYTES = 1
GRANT = 55900000
PIECES = 2


def call(name, body, outs, *args, flops=0, ins=None, to=None, aliases=None, scratch=(), grant=32 << 20):
    size = sum(a.size * a.dtype.itemsize for a in args) + sum(
        math.prod(s) * jnp.dtype(t).itemsize for s, t in outs
    )
    return pl.pallas_call(
        body,
        name=name,
        out_shape=[jax.ShapeDtypeStruct(s, t) for s, t in outs],
        in_specs=ins or [VMEM] * len(args),
        out_specs=to or [VMEM] * len(outs),
        scratch_shapes=scratch,
        input_output_aliases=aliases or {},
        compiler_params=pltpu.CompilerParams(vmem_limit_bytes=grant),
        cost_estimate=pl.CostEstimate(flops=int(flops), bytes_accessed=int(size * BYTES), transcendentals=0),
    )(*args)


def load_kernel(x_hbm, *refs):
    outs, sem = refs[:2], refs[2]
    half = outs[0].shape[-1]
    pieces = sem.shape[0]
    rows = x_hbm.shape[0] // pieces
    copies = []
    for side in (1, 0):
        for i in range(pieces):
            at = pl.ds(i * rows, rows)
            from_ref = x_hbm.at[at, :, pl.ds(side * half, half)]
            copies.append(pltpu.make_async_copy(from_ref, outs[side].at[at], sem.at[i, side]))
            copies[-1].start()
    for copy in copies:
        copy.wait()


def part_kernel(x_ref, out_ref):
    out_ref[...] = jnp.swapaxes(x_ref[...], 0, 1)


def prep_kernel(x_hbm, qg_ref, kg_ref, _, __, keep_ref, send_ref, buf, sem):
    width = keep_ref.shape[-1]
    first = lax.axis_index("uly") == 0
    copies = [pltpu.make_async_copy(x_hbm.at[i], buf.at[i], sem.at[i]) for i in range(3)]
    for copy in copies:
        copy.start()

    def put(part, rows):
        low, high = rows[:, :width], rows[:, width:]

        @pl.when(first)
        def _():
            keep_ref[part] = low
            send_ref[part] = high

        @pl.when(jnp.logical_not(first))
        def _():
            keep_ref[part] = high
            send_ref[part] = low

    for part, gain in ((0, qg_ref), (1, kg_ref)):
        copies[part].wait()
        rows = buf[part].astype(F32)
        inverse = lax.rsqrt(jnp.mean(rows * rows, axis=-1, keepdims=True) + EPSILON)
        put(part, (rows * inverse * gain[...]).astype(BF16))
    copies[2].wait()
    put(2, buf[2])


def scores_of(query, key):
    return lax.dot_general(query, key, (((1,), (1,)), ((), ())), preferred_element_type=F32)


def both(one, two):
    return jnp.concatenate([one.astype(F32), two.astype(F32)], axis=0).astype(BF16)


def weigh(scores, old):
    top = jnp.max(functools.reduce(jnp.maximum, scores), axis=-1, keepdims=True)
    if old is None:
        weights = [jnp.exp2((s - top) * SCALE) for s in scores]
        total = jnp.sum(functools.reduce(jnp.add, weights), axis=-1, keepdims=True)
        shape = (top.shape[0], HD)
        return weights, None, jnp.broadcast_to(top, shape), jnp.broadcast_to(total, shape)
    _, best, total = old
    new = jnp.maximum(best, jnp.broadcast_to(top, best.shape))
    shrink = jnp.exp2((best - new) * SCALE)
    weights = [jnp.exp2((s - new[:, : s.shape[-1]]) * SCALE) for s in scores]
    total = total * shrink + jnp.sum(functools.reduce(jnp.add, weights), axis=-1, keepdims=True)
    return weights, shrink, new, total


def attend(heads):
    scores = [[scores_of(query, key) for key in keys] for query, keys, _, _ in heads]
    weighed = [weigh(s, old) for s, (_, _, _, old) in zip(scores, heads)]
    for (_, _, values, old), (weights, shrink, best, total) in zip(heads, weighed):
        products = [
            jnp.dot(w.astype(BF16), value, preferred_element_type=F32)
            for w, value in zip(weights, values)
        ]
        acc = functools.reduce(jnp.add, products)
        yield (acc if old is None else old[0] * shrink + acc), best, total


def own_kernel(keep_ref, recv_ref, *outs):
    count = outs[0].shape[-1] // HD
    heads = []
    for head in range(2 * count):
        at = pl.ds(head * HD, HD)
        query, key, value = (both(keep_ref[i, :, at], recv_ref[i, :, at]) for i in range(3))
        heads.append((query, [key], [value], None))
    for head, new in enumerate(attend(heads)):
        q_ref, *state = outs[4 * (head // count) : 4 * (head // count) + 4]
        to = pl.ds(head % count * HD, HD)
        q_ref[:, to] = heads[head][0]
        for ref, value in zip(state, new):
            ref[:, to] = value


def update_kernel(blocks, q_ref, *refs):
    kv_refs, state, outs = refs[:blocks], refs[blocks : blocks + 3], refs[blocks + 3 :]
    heads = []
    for head in range(q_ref.shape[-1] // HD):
        at = pl.ds(head * HD, HD)
        keys, values = ([kv[i, :, at] for kv in kv_refs] for i in range(2))
        heads.append((q_ref[:, at], keys, values, [ref[:, at] for ref in state]))
    for head, new in enumerate(attend(heads)):
        for ref, value in zip(outs, new):
            ref[:, head * HD : (head + 1) * HD] = value


def finish(begin, q_ref, sides, out_ref, skip=0):
    rows = q_ref.shape[1]
    skip *= out_ref.shape[-1] // HD
    heads = []
    for *state, kv_refs in sides:
        for head in range(state[0].shape[-1] // HD):
            at = pl.ds(head * HD, HD)
            query = q_ref[0, :, pl.ds((skip + len(heads)) * HD, HD)]
            keys, values = ([kv[i, :, at] for kv in kv_refs] for i in range(2))
            old = [ref[begin : begin + rows, at] for ref in state]
            heads.append((query, keys, values, old))
    for head, (acc, _, total) in enumerate(attend(heads)):
        out_ref[:, head * HD : (head + 1) * HD] = (acc / total).astype(BF16)


def two_sides(refs, cut):
    return [(*side[:3], side[3:]) for side in (refs[:cut], refs[cut:])]


def send_kernel(begin, side, q_ref, *refs):
    finish(begin, q_ref, [(*refs[:3], refs[3:-1])], refs[-1], side)


def mine_kernel(begin, cut, q_ref, *refs):
    finish(begin, q_ref, two_sides(refs[:-1], cut), refs[-1])


def join_kernel(mine_ref, one_ref, two_ref, out_hbm, sem):
    here = lax.axis_index("uly")
    width, half = mine_ref.shape[-1], one_ref.shape[-1]
    starts = [here * width, (1 - here) * width, (1 - here) * width + half]
    copies = []
    for i, (start, ref) in enumerate(zip(starts, (mine_ref, one_ref, two_ref))):
        at = pl.ds(pl.multiple_of(start, HD), ref.shape[-1])
        copies.append(pltpu.make_async_copy(ref, out_hbm.at[:, at], sem.at[i]))
        copies[i].start()
    for copy in copies:
        copy.wait()


def shards(n, fresh_qkv, stale_kv, q_gain, k_gain):
    rows, _, features = fresh_qkv.shape
    patch_rows, _, width = stale_kv.shape
    half = width // 2
    around = list(range(0, n, 2)) + list(range(1, n, 2))[::-1]
    right = [(around[i], around[(i + 1) % n]) for i in range(n)]
    left = [(b, a) for a, b in right]
    swap = [(0, 1), (1, 0)]
    far, near = n // 2, (n - 1) // 2

    dma = pltpu.SemaphoreType.DMA
    sides = call(
        "load",
        load_kernel,
        [((patch_rows, 2, half), BF16)] * 2,
        stale_kv,
        ins=[ANY],
        scratch=[dma((PIECES, 2))],
        grant=GRANT,
    )
    forward, backward = list(sides), list(sides)
    arrived = [[], []]
    def move(block, hop, way):
        block = lax.ppermute(block, "patch", way)
        return call("part", part_kernel, [((2, patch_rows, half), BF16)], block)[0] if hop == 0 else block

    for hop in range(max(far, near)):
        for side in range(2):
            got = []
            if hop < (far if side == 0 else near):
                forward[side] = move(forward[side], hop, right)
                got.append(forward[side])
            if hop < (near if side == 0 else far):
                backward[side] = move(backward[side], hop, left)
                got.append(backward[side])
            arrived[side].append(got)

    keep, send = call(
        "prep",
        prep_kernel,
        [((3, rows, width), BF16)] * 2,
        fresh_qkv.transpose(1, 0, 2),
        q_gain.reshape(1, features),
        k_gain.reshape(1, features),
        *sides,
        ins=[ANY, VMEM, VMEM, ANY, ANY],
        scratch=[pltpu.VMEM((3, rows, features), BF16), dma((3,))],
        flops=PREP * patch_rows * patch_rows * width // 8,
    )
    recv = lax.ppermute(send, "uly", swap)
    state = [((patch_rows, half), F32)] * 3
    work = WORK * 4 * patch_rows * patch_rows * half
    own = call("own", own_kernel, ([((patch_rows, half), BF16)] + state) * 2, keep, recv, flops=OWN * work)
    queries = [own[0], own[4]]
    states = [own[1:4], own[5:8]]
    for hop in range(len(arrived[0]) - 1):
        for side in range(2):
            blocks = arrived[side][hop]
            body = functools.partial(update_kernel, len(blocks))
            states[side] = call(
                f"update{hop}{side}", body, state, queries[side], *blocks, *states[side], flops=len(blocks) * (work if hop < len(arrived[0]) - 2 else LATE * work)
            )
    incoming = [None, None]
    for side in (1, 0):
        (outgoing,) = call(
            f"send{side}",
            functools.partial(send_kernel, rows, side),
            [((rows, half), BF16)],
            recv,
            *states[side],
            *arrived[side][-1],
            flops=work // 2,
        )
        incoming[side] = lax.ppermute(outgoing, "uly", swap)
    last = [*states[0], *arrived[0][-1], *states[1], *arrived[1][-1]]
    cut = len(states[0]) + len(arrived[0][-1])
    (mine,) = call(
        "mine", functools.partial(mine_kernel, 0, cut), [((rows, width), BF16)], keep, *last, flops=work
    )
    (out,) = call(
        "join",
        join_kernel,
        [((rows, features), BF16)],
        mine,
        *incoming,
        to=[ANY],
        scratch=[dma((3,))],
    )
    return out


def solution(mesh):
    in_specs = (
        P(("groups", "patch", "uly"), None, None),
        P(("groups", "patch"), None, "uly"),
        P(),
        P(),
    )
    out_specs = P(("groups", "patch", "uly"), None)
    body = functools.partial(shards, mesh.shape["patch"])
    return jax.shard_map(body, mesh=mesh, in_specs=in_specs, out_specs=out_specs, check_vma=False)
```

```python
import functools
import math

import jax
import jax.numpy as jnp
from jax import lax
from jax.experimental import pallas as pl
from jax.experimental.pallas import tpu as pltpu
from jax.sharding import PartitionSpec as P

HD = 128
EPSILON = 1e-06
SCALE = math.log2(math.e) / math.sqrt(HD)
VMEM = pl.BlockSpec(memory_space=pltpu.VMEM)
ANY = pl.BlockSpec(memory_space=pl.ANY)
F32 = jnp.float32
BF16 = jnp.bfloat16
WORK = 1
OWN = 1
LATE = 1
PREP = 1
BYTES = 1
GRANT = 55900000
PIECES = 5


def call(name, body, outs, *args, flops=0, ins=None, to=None, aliases=None, scratch=(), grant=32 << 20):
    size = sum(a.size * a.dtype.itemsize for a in args) + sum(
        math.prod(s) * jnp.dtype(t).itemsize for s, t in outs
    )
    return pl.pallas_call(
        body,
        name=name,
        out_shape=[jax.ShapeDtypeStruct(s, t) for s, t in outs],
        in_specs=ins or [VMEM] * len(args),
        out_specs=to or [VMEM] * len(outs),
        scratch_shapes=scratch,
        input_output_aliases=aliases or {},
        compiler_params=pltpu.CompilerParams(vmem_limit_bytes=grant),
        cost_estimate=pl.CostEstimate(flops=int(flops), bytes_accessed=int(size * BYTES), transcendentals=0),
    )(*args)


def load_kernel(x_hbm, *refs):
    outs, sem = refs[:2], refs[2]
    half = outs[0].shape[-1]
    copies = []
    for side in range(2):
        at = pl.ds(side * half, half)
        copies.append(pltpu.make_async_copy(x_hbm.at[:, :, at], outs[side], sem.at[side]))
        copies[side].start()
    for copy in copies:
        copy.wait()


def part_kernel(x_ref, out_ref):
    out_ref[...] = jnp.swapaxes(x_ref[...], 0, 1)


def prep_kernel(x_ref, qg_ref, kg_ref, _, __, keep_ref, send_ref):
    width = keep_ref.shape[-1]
    first = lax.axis_index("uly") == 0

    def put(part, rows):
        low, high = rows[:, :width], rows[:, width:]

        @pl.when(first)
        def _():
            keep_ref[part] = low
            send_ref[part] = high

        @pl.when(jnp.logical_not(first))
        def _():
            keep_ref[part] = high
            send_ref[part] = low

    for part, gain in ((0, qg_ref), (1, kg_ref)):
        rows = x_ref[part].astype(F32)
        inverse = lax.rsqrt(jnp.mean(rows * rows, axis=-1, keepdims=True) + EPSILON)
        put(part, (rows * inverse * gain[...]).astype(BF16))
    put(2, x_ref[2])


def scores_of(query, key):
    return lax.dot_general(query, key, (((1,), (1,)), ((), ())), preferred_element_type=F32)


def both(one, two):
    return jnp.concatenate([one.astype(F32), two.astype(F32)], axis=0).astype(BF16)


def weigh(scores, old):
    top = jnp.max(functools.reduce(jnp.maximum, scores), axis=-1, keepdims=True)
    if old is None:
        weights = [jnp.exp2((s - top) * SCALE) for s in scores]
        total = jnp.sum(functools.reduce(jnp.add, weights), axis=-1, keepdims=True)
        shape = (top.shape[0], HD)
        return weights, None, jnp.broadcast_to(top, shape), jnp.broadcast_to(total, shape)
    _, best, total = old
    new = jnp.maximum(best, jnp.broadcast_to(top, best.shape))
    shrink = jnp.exp2((best - new) * SCALE)
    weights = [jnp.exp2((s - new[:, : s.shape[-1]]) * SCALE) for s in scores]
    total = total * shrink + jnp.sum(functools.reduce(jnp.add, weights), axis=-1, keepdims=True)
    return weights, shrink, new, total


def attend(heads):
    scores = [[scores_of(query, key) for key in keys] for query, keys, _, _ in heads]
    weighed = [weigh(s, old) for s, (_, _, _, old) in zip(scores, heads)]
    for (_, _, values, old), (weights, shrink, best, total) in zip(heads, weighed):
        products = [
            jnp.dot(w.astype(BF16), value, preferred_element_type=F32)
            for w, value in zip(weights, values)
        ]
        acc = functools.reduce(jnp.add, products)
        yield (acc if old is None else old[0] * shrink + acc), best, total


def own_kernel(keep_ref, recv_ref, *outs):
    count = outs[0].shape[-1] // HD
    heads = []
    for head in range(2 * count):
        at = pl.ds(head * HD, HD)
        query, key, value = (both(keep_ref[i, :, at], recv_ref[i, :, at]) for i in range(3))
        heads.append((query, [key], [value], None))
    for head, new in enumerate(attend(heads)):
        q_ref, *state = outs[4 * (head // count) : 4 * (head // count) + 4]
        to = pl.ds(head % count * HD, HD)
        q_ref[:, to] = heads[head][0]
        for ref, value in zip(state, new):
            ref[:, to] = value


def update_kernel(blocks, q_ref, *refs):
    kv_refs, state, outs = refs[:blocks], refs[blocks : blocks + 3], refs[blocks + 3 :]
    heads = []
    for head in range(q_ref.shape[-1] // HD):
        at = pl.ds(head * HD, HD)
        keys, values = ([kv[i, :, at] for kv in kv_refs] for i in range(2))
        heads.append((q_ref[:, at], keys, values, [ref[:, at] for ref in state]))
    for head, new in enumerate(attend(heads)):
        for ref, value in zip(outs, new):
            ref[:, head * HD : (head + 1) * HD] = value


def finish(begin, q_ref, sides, out_ref):
    rows = q_ref.shape[1]
    heads = []
    for *state, kv_refs in sides:
        for head in range(state[0].shape[-1] // HD):
            at = pl.ds(head * HD, HD)
            query = q_ref[0, :, pl.ds(len(heads) * HD, HD)]
            keys, values = ([kv[i, :, at] for kv in kv_refs] for i in range(2))
            old = [ref[begin : begin + rows, at] for ref in state]
            heads.append((query, keys, values, old))
    for head, (acc, _, total) in enumerate(attend(heads)):
        out_ref[:, head * HD : (head + 1) * HD] = (acc / total).astype(BF16)


def two_sides(refs, cut):
    return [(*side[:3], side[3:]) for side in (refs[:cut], refs[cut:])]


def send_kernel(begin, cut, q_ref, *refs):
    finish(begin, q_ref, two_sides(refs[:-1], cut), refs[-1])


def mine_kernel(begin, cut, q_ref, *refs):
    finish(begin, q_ref, two_sides(refs[:-1], cut), refs[-1])


def join_kernel(mine_ref, recv_ref, out_hbm, sem):
    here = lax.axis_index("uly")
    width = mine_ref.shape[-1]
    copies = []
    for i, (place, ref) in enumerate(((here, mine_ref), (1 - here, recv_ref))):
        at = pl.ds(pl.multiple_of(place * width, HD), width)
        copies.append(pltpu.make_async_copy(ref, out_hbm.at[:, at], sem.at[i]))
        copies[i].start()
    for copy in copies:
        copy.wait()


def shards(n, fresh_qkv, stale_kv, q_gain, k_gain):
    rows, _, features = fresh_qkv.shape
    patch_rows, _, width = stale_kv.shape
    half = width // 2
    around = list(range(0, n, 2)) + list(range(1, n, 2))[::-1]
    right = [(around[i], around[(i + 1) % n]) for i in range(n)]
    left = [(b, a) for a, b in right]
    ways = [
        [(2 * a + core, 2 * b + core) for core, way in enumerate(pair) for a, b in way]
        for pair in ((left, right), (right, left))
    ]
    swap = [(0, 1), (1, 0)]
    far, near = n // 2, (n - 1) // 2

    dma = pltpu.SemaphoreType.DMA
    sides = call(
        "load",
        load_kernel,
        [((patch_rows, 2, half), BF16)] * 2,
        stale_kv,
        ins=[ANY],
        scratch=[dma((2,))],
        grant=GRANT,
    )
    forward, backward = list(sides), list(sides)
    arrived = [[], []]
    def move(block, hop, way):
        block = lax.ppermute(block, ("patch", "uly"), way)
        return call("part", part_kernel, [((2, patch_rows, half), BF16)], block)[0] if hop == 0 else block

    for hop in range(max(far, near)):
        for side in range(2):
            got = []
            if hop < (far if side == 0 else near):
                forward[side] = move(forward[side], hop, ways[0])
                got.append(forward[side])
            if hop < (near if side == 0 else far):
                backward[side] = move(backward[side], hop, ways[1])
                got.append(backward[side])
            arrived[side].append(got)

    keep, send = call(
        "prep",
        prep_kernel,
        [((3, rows, width), BF16)] * 2,
        fresh_qkv.transpose(1, 0, 2),
        q_gain.reshape(1, features),
        k_gain.reshape(1, features),
        *sides,
        ins=[VMEM, VMEM, VMEM, ANY, ANY],
        flops=PREP * patch_rows * patch_rows * width // 8,
    )
    recv = lax.ppermute(send, "uly", swap)
    state = [((patch_rows, half), F32)] * 3
    work = WORK * 4 * patch_rows * patch_rows * half
    own = call("own", own_kernel, ([((patch_rows, half), BF16)] + state) * 2, keep, recv, flops=OWN * work)
    queries = [own[0], own[4]]
    states = [own[1:4], own[5:8]]
    for hop in range(len(arrived[0]) - 1):
        for side in range(2):
            blocks = arrived[side][hop]
            body = functools.partial(update_kernel, len(blocks))
            states[side] = call(
                f"update{hop}{side}", body, state, queries[side], *blocks, *states[side], flops=len(blocks) * (work if hop < len(arrived[0]) - 2 else LATE * work)
            )
    last = [*states[0], *arrived[0][-1], *states[1], *arrived[1][-1]]
    cut = len(states[0]) + len(arrived[0][-1])
    (outgoing,) = call(
        "send", functools.partial(send_kernel, rows, cut), [((rows, width), BF16)], recv, *last, flops=work
    )
    incoming = lax.ppermute(outgoing, "uly", swap)
    (mine,) = call(
        "mine", functools.partial(mine_kernel, 0, cut), [((rows, width), BF16)], keep, *last, flops=work
    )
    (out,) = call(
        "join",
        join_kernel,
        [((rows, features), BF16)],
        mine,
        incoming,
        to=[ANY],
        scratch=[dma((2,))],
    )
    return out


def solution(mesh):
    in_specs = (
        P(("groups", "patch", "uly"), None, None),
        P(("groups", "patch"), None, "uly"),
        P(),
        P(),
    )
    out_specs = P(("groups", "patch", "uly"), None)
    body = functools.partial(shards, mesh.shape["patch"])
    return jax.shard_map(body, mesh=mesh, in_specs=in_specs, out_specs=out_specs, check_vma=False)
```

```python
import functools
import math

import jax
import jax.numpy as jnp
from jax import lax
from jax.experimental import pallas as pl
from jax.experimental.pallas import tpu as pltpu
from jax.sharding import PartitionSpec as P

HD = 128
EPSILON = 1e-06
SCALE = math.log2(math.e) / math.sqrt(HD)
VMEM = pl.BlockSpec(memory_space=pltpu.VMEM)
ANY = pl.BlockSpec(memory_space=pl.ANY)
F32 = jnp.float32
BF16 = jnp.bfloat16
WORK = 1
OWN = 1
LATE = 1
PREP = 1
BYTES = 1
GRANT = 55900000
PIECES = 5


def call(name, body, outs, *args, flops=0, ins=None, to=None, aliases=None, scratch=(), grant=32 << 20):
    size = sum(a.size * a.dtype.itemsize for a in args) + sum(
        math.prod(s) * jnp.dtype(t).itemsize for s, t in outs
    )
    return pl.pallas_call(
        body,
        name=name,
        out_shape=[jax.ShapeDtypeStruct(s, t) for s, t in outs],
        in_specs=ins or [VMEM] * len(args),
        out_specs=to or [VMEM] * len(outs),
        scratch_shapes=scratch,
        input_output_aliases=aliases or {},
        compiler_params=pltpu.CompilerParams(vmem_limit_bytes=grant),
        cost_estimate=pl.CostEstimate(flops=int(flops), bytes_accessed=int(size * BYTES), transcendentals=0),
    )(*args)


def load_kernel(x_hbm, *refs):
    outs, sem = refs[:2], refs[2]
    half = outs[0].shape[-1]
    copies = []
    for side in range(2):
        at = pl.ds(side * half, half)
        copies.append(pltpu.make_async_copy(x_hbm.at[:, :, at], outs[side], sem.at[side]))
        copies[side].start()
    for copy in copies:
        copy.wait()


def part_kernel(x_ref, out_ref):
    out_ref[...] = jnp.swapaxes(x_ref[...], 0, 1)


def prep_kernel(x_ref, qg_ref, kg_ref, _, __, keep_ref, send_ref):
    width = keep_ref.shape[-1]
    first = lax.axis_index("uly") == 0

    def put(part, rows):
        low, high = rows[:, :width], rows[:, width:]

        @pl.when(first)
        def _():
            keep_ref[part] = low
            send_ref[part] = high

        @pl.when(jnp.logical_not(first))
        def _():
            keep_ref[part] = high
            send_ref[part] = low

    for part, gain in ((0, qg_ref), (1, kg_ref)):
        rows = x_ref[part].astype(F32)
        inverse = lax.rsqrt(jnp.mean(rows * rows, axis=-1, keepdims=True) + EPSILON)
        put(part, (rows * inverse * gain[...]).astype(BF16))
    put(2, x_ref[2])


def scores_of(query, key):
    return lax.dot_general(query, key, (((1,), (1,)), ((), ())), preferred_element_type=F32)


def both(one, two):
    return jnp.concatenate([one.astype(F32), two.astype(F32)], axis=0).astype(BF16)


def weigh(scores, old):
    top = jnp.max(functools.reduce(jnp.maximum, scores), axis=-1, keepdims=True)
    if old is None:
        weights = [jnp.exp2((s - top) * SCALE) for s in scores]
        total = jnp.sum(functools.reduce(jnp.add, weights), axis=-1, keepdims=True)
        shape = (top.shape[0], HD)
        return weights, None, jnp.broadcast_to(top, shape), jnp.broadcast_to(total, shape)
    _, best, total = old
    new = jnp.maximum(best, jnp.broadcast_to(top, best.shape))
    shrink = jnp.exp2((best - new) * SCALE)
    weights = [jnp.exp2((s - new[:, : s.shape[-1]]) * SCALE) for s in scores]
    total = total * shrink + jnp.sum(functools.reduce(jnp.add, weights), axis=-1, keepdims=True)
    return weights, shrink, new, total


def attend(heads):
    scores = [[scores_of(query, key) for key in keys] for query, keys, _, _ in heads]
    weighed = [weigh(s, old) for s, (_, _, _, old) in zip(scores, heads)]
    for (_, _, values, old), (weights, shrink, best, total) in zip(heads, weighed):
        products = [
            jnp.dot(w.astype(BF16), value, preferred_element_type=F32)
            for w, value in zip(weights, values)
        ]
        acc = functools.reduce(jnp.add, products)
        yield (acc if old is None else old[0] * shrink + acc), best, total


def own_kernel(keep_ref, recv_ref, *outs):
    count = outs[0].shape[-1] // HD
    heads = []
    for head in range(2 * count):
        at = pl.ds(head * HD, HD)
        query, key, value = (both(keep_ref[i, :, at], recv_ref[i, :, at]) for i in range(3))
        heads.append((query, [key], [value], None))
    for head, new in enumerate(attend(heads)):
        q_ref, *state = outs[4 * (head // count) : 4 * (head // count) + 4]
        to = pl.ds(head % count * HD, HD)
        q_ref[:, to] = heads[head][0]
        for ref, value in zip(state, new):
            ref[:, to] = value


def update_kernel(blocks, q_ref, *refs):
    kv_refs, state, outs = refs[:blocks], refs[blocks : blocks + 3], refs[blocks + 3 :]
    heads = []
    for head in range(q_ref.shape[-1] // HD):
        at = pl.ds(head * HD, HD)
        keys, values = ([kv[i, :, at] for kv in kv_refs] for i in range(2))
        heads.append((q_ref[:, at], keys, values, [ref[:, at] for ref in state]))
    for head, new in enumerate(attend(heads)):
        for ref, value in zip(outs, new):
            ref[:, head * HD : (head + 1) * HD] = value


def finish(begin, q_ref, sides, out_ref):
    rows = q_ref.shape[1]
    heads = []
    for *state, kv_refs in sides:
        for head in range(state[0].shape[-1] // HD):
            at = pl.ds(head * HD, HD)
            query = q_ref[0, :, pl.ds(len(heads) * HD, HD)]
            keys, values = ([kv[i, :, at] for kv in kv_refs] for i in range(2))
            old = [ref[begin : begin + rows, at] for ref in state]
            heads.append((query, keys, values, old))
    for head, (acc, _, total) in enumerate(attend(heads)):
        out_ref[:, head * HD : (head + 1) * HD] = (acc / total).astype(BF16)


def two_sides(refs, cut):
    return [(*side[:3], side[3:]) for side in (refs[:cut], refs[cut:])]


def send_kernel(begin, cut, q_ref, *refs):
    finish(begin, q_ref, two_sides(refs[:-1], cut), refs[-1])


def mine_kernel(begin, cut, q_ref, *refs):
    finish(begin, q_ref, two_sides(refs[:-1], cut), refs[-1])


def join_kernel(mine_ref, recv_ref, out_hbm, sem):
    here = lax.axis_index("uly")
    width = mine_ref.shape[-1]
    copies = []
    for i, (place, ref) in enumerate(((here, mine_ref), (1 - here, recv_ref))):
        at = pl.ds(pl.multiple_of(place * width, HD), width)
        copies.append(pltpu.make_async_copy(ref, out_hbm.at[:, at], sem.at[i]))
        copies[i].start()
    for copy in copies:
        copy.wait()


def shards(n, fresh_qkv, stale_kv, q_gain, k_gain):
    rows, _, features = fresh_qkv.shape
    patch_rows, _, width = stale_kv.shape
    half = width // 2
    around = list(range(0, n, 2)) + list(range(1, n, 2))[::-1]
    right = [(around[i], around[(i + 1) % n]) for i in range(n)]
    left = [(b, a) for a, b in right]
    ways = [
        [(2 * a + core, 2 * b + core) for core, way in enumerate(pair) for a, b in way]
        for pair in ((right, left), (left, right))
    ]
    swap = [(0, 1), (1, 0)]
    far, near = n // 2, (n - 1) // 2

    dma = pltpu.SemaphoreType.DMA
    sides = call(
        "load",
        load_kernel,
        [((patch_rows, 2, half), BF16)] * 2,
        stale_kv,
        ins=[ANY],
        scratch=[dma((2,))],
        grant=GRANT,
    )
    forward, backward = list(sides), list(sides)
    arrived = [[], []]
    def move(block, hop, way):
        block = lax.ppermute(block, ("patch", "uly"), way)
        return call("part", part_kernel, [((2, patch_rows, half), BF16)], block)[0] if hop == 0 else block

    for hop in range(max(far, near)):
        for side in range(2):
            got = []
            if hop < (far if side == 0 else near):
                forward[side] = move(forward[side], hop, ways[0])
                got.append(forward[side])
            if hop < (near if side == 0 else far):
                backward[side] = move(backward[side], hop, ways[1])
                got.append(backward[side])
            arrived[side].append(got)

    keep, send = call(
        "prep",
        prep_kernel,
        [((3, rows, width), BF16)] * 2,
        fresh_qkv.transpose(1, 0, 2),
        q_gain.reshape(1, features),
        k_gain.reshape(1, features),
        *sides,
        ins=[VMEM, VMEM, VMEM, ANY, ANY],
        flops=PREP * patch_rows * patch_rows * width // 8,
    )
    recv = lax.ppermute(send, "uly", swap)
    state = [((patch_rows, half), F32)] * 3
    work = WORK * 4 * patch_rows * patch_rows * half
    own = call("own", own_kernel, ([((patch_rows, half), BF16)] + state) * 2, keep, recv, flops=OWN * work)
    queries = [own[0], own[4]]
    states = [own[1:4], own[5:8]]
    for hop in range(len(arrived[0]) - 1):
        for side in range(2):
            blocks = arrived[side][hop]
            body = functools.partial(update_kernel, len(blocks))
            states[side] = call(
                f"update{hop}{side}", body, state, queries[side], *blocks, *states[side], flops=len(blocks) * (work if hop < len(arrived[0]) - 2 else LATE * work)
            )
    last = [*states[0], *arrived[0][-1], *states[1], *arrived[1][-1]]
    cut = len(states[0]) + len(arrived[0][-1])
    (outgoing,) = call(
        "send", functools.partial(send_kernel, rows, cut), [((rows, width), BF16)], recv, *last, flops=work
    )
    incoming = lax.ppermute(outgoing, "uly", swap)
    (mine,) = call(
        "mine", functools.partial(mine_kernel, 0, cut), [((rows, width), BF16)], keep, *last, flops=work
    )
    (out,) = call(
        "join",
        join_kernel,
        [((rows, features), BF16)],
        mine,
        incoming,
        to=[ANY],
        scratch=[dma((2,))],
    )
    return out


def solution(mesh):
    in_specs = (
        P(("groups", "patch", "uly"), None, None),
        P(("groups", "patch"), None, "uly"),
        P(),
        P(),
    )
    out_specs = P(("groups", "patch", "uly"), None)
    body = functools.partial(shards, mesh.shape["patch"])
    return jax.shard_map(body, mesh=mesh, in_specs=in_specs, out_specs=out_specs, check_vma=False)
```
